128 devices in a mesh: row: 32 (over y, z, x_lo), col: 4 (over x_hi, core).
Axes of the slice: x: 4 (x_hi: 2, x_lo: 2; x = x_hi * 2 + x_lo), y: 4, z: 4, core: 2. Of those that a mesh axis runs over, the one named last changes fastest.
Arguments:
- amp_first: bfloat16 [512, 65536], P('col', 'row'), may hold values from -6 to 6
- amp_second: bfloat16 [512, 16384], P('row', 'col'), may hold values from -6 to 6
- integrals: bfloat16 [65536, 16384], P('row', 'col'), may hold values from -0.0234375 to 0.0234375
- tile_order: int32 [4, 16], P('col'), may hold values from 0 to 15, each once within a row
Outputs:
- ladder_first: bfloat16 [512, 65536], P('col', 'row')
- ladder_second: bfloat16 [512, 16384], P('row', 'col')
The draws below stay inside these ranges and needn't reach their ends.
Inputs may be any that keep to these rules, and one draw needn't show every extreme that they name: Each row of tile_order holds every number from 0 to 15 once.
All inputs are finite; a program needn't handle non-finite values.
Results may differ from the reference program's by a relative error of at most 0.001.
Values may be sent and summed in bfloat16 or wider, within the bound.
No kernel may reach another device: no remote copies, remote signals or barrier semaphores. Data moves between devices by JAX's collectives and lax.ppermute only.
A program may use at most 128 MiB of HBM per device.

```python
import jax
import jax.numpy as jnp
from jax import lax

TILE = 256
OCC = 512
CT = 16
NA = 65536
NB = 16384
N_COL = 4


def block_levels(own_key, extent, pieces, low, high):
    factor_of = 1.0
    for position, blocks in pieces:
        heights = jax.random.uniform(jax.random.fold_in(jax.random.fold_in(own_key, 6), position), (blocks,), jnp.float32, low / len(pieces), high / len(pieces))
        factor_of = factor_of * jnp.repeat(jnp.exp(heights), extent[position] // blocks).reshape((-1,) + (1,) * (len(extent) - 1 - position))
    return factor_of


def noise(stream_key, dims, deviation, reach, cuts=(), dtype=jnp.bfloat16):
    values = deviation * jax.random.normal(stream_key, dims, jnp.float32)
    if cuts:
        values = values * block_levels(stream_key, dims, cuts, -0.22, 0.18)
    return jnp.clip(values, -reach, reach).astype(dtype)


def setup_inputs(seed: int = 0) -> dict:
    arg_keys = jax.random.split(jax.random.key(seed), 5)
    return {
        "amp_first": noise(arg_keys[0], (OCC, NA), 1.0, 6.0, ((0, 4), (1, 32))),
        "amp_second": noise(arg_keys[1], (OCC, NB), 1.0, 6.0, ((0, 32), (1, 4))),
        "integrals": noise(arg_keys[2], (NA, NB), NA ** -0.5, 0.0234375, ((0, 32), (1, 4))),
        "tile_order": jax.vmap(lambda own: jax.random.permutation(own, CT))(jax.random.split(arg_keys[3], N_COL)).reshape((N_COL, CT)).astype(jnp.int32),
    }


def reference(amp_first, amp_second, integrals, tile_order):
    tiles = amp_second.reshape(OCC, N_COL, CT, TILE)
    paired = jnp.take_along_axis(tiles, tile_order.astype(jnp.int32)[None, :, :, None], axis=2).reshape(OCC, NB)
    first = lax.dot_general(paired, integrals, (((1,), (1,)), ((), ())), preferred_element_type=jnp.float32)
    second = jnp.dot(amp_first, integrals, preferred_element_type=jnp.float32)
    return first.astype(jnp.bfloat16), second.astype(jnp.bfloat16)
```

```python
import functools

import jax
import jax.numpy as jnp
from jax import lax
from jax.experimental import pallas as pl
from jax.experimental.pallas import tpu as pltpu
from jax.sharding import PartitionSpec as P

F32, BF16 = jnp.float32, jnp.bfloat16
TILE = 256
OCC, NA_D, NB_D, CT = 512, 2048, 4096, 16
TN = 512
HALF = NB_D // 2
VMEM_LIMIT = 28 * 2**20


def exchange_pairs(y=0, z=0, xl=0, xh=0, core=0):
    row_flip = y * 8 + z * 2 + xl
    col_flip = xh * 2 + core
    return [
        (row * 4 + col, (row ^ row_flip) * 4 + (col ^ col_flip))
        for row in range(32)
        for col in range(4)
    ]


def swap(value, **flips):
    return lax.ppermute(value, ("row", "col"), exchange_pairs(**flips))


def cost(flops, moved):
    return pl.CostEstimate(flops=flops, bytes_accessed=moved, transcendentals=0)


def call(kernel, grid, scalars, operands, in_specs, outs, scratch, flops, name):
    out_specs = [spec for spec, _ in outs]
    out_shape = [shape for _, shape in outs]
    moved = sum(a.size * a.dtype.itemsize for a in operands) + sum(
        s.size * s.dtype.itemsize for s in out_shape
    )
    return pl.pallas_call(
        kernel,
        grid_spec=pltpu.PrefetchScalarGridSpec(
            num_scalar_prefetch=1,
            grid=grid,
            in_specs=in_specs,
            out_specs=out_specs,
            scratch_shapes=scratch,
        ),
        out_shape=out_shape,
        compiler_params=pltpu.CompilerParams(vmem_limit_bytes=VMEM_LIMIT),
        cost_estimate=cost(flops, moved),
        name=name,
    )(scalars, *operands)


def whole(shape):
    return pl.BlockSpec(shape, lambda i, s: (0,) * len(shape))


def mirror_kernel(y_first, start, s_ref, f0, f1, f2, f3, i_ref, o0, o1, o2, o3, lhs):
    y_col, z_xl = s_ref[0], s_ref[1]

    @pl.when(pl.program_id(0) == 0)
    def _():
        for rel_col, f in enumerate((f0, f1, f2, f3)):
            rel_y = rel_col ^ y_col
            for zx in range(8):
                rel = zx ^ z_xl
                if y_first:
                    slot = rel_y * 8 + rel
                else:
                    slot = ((rel >> 1) * 4 + rel_y) * 2 + (rel & 1)
                lhs[pl.ds(pl.multiple_of(slot * 16, 16), 16), :] = f[zx * 16 : zx * 16 + 16]

    column = pl.multiple_of(start + pl.program_id(0) * TN, TN)
    sums = jnp.dot(lhs[...], i_ref[:, pl.ds(column, TN)], preferred_element_type=F32)
    for k, o in enumerate((o0, o1, o2, o3)):
        o[...] = sums[k * 128 : k * 128 + 128]


def mirror(scalars, firsts, integrals, y_first, start):
    out = (pl.BlockSpec((128, TN), lambda i, s: (0, i)), jax.ShapeDtypeStruct((128, HALF), F32))
    return call(
        functools.partial(mirror_kernel, y_first, start),
        (HALF // TN,),
        scalars,
        (*firsts, integrals),
        [whole((128, NA_D))] * 4 + [pl.BlockSpec(memory_space=pltpu.VMEM)],
        [out] * 4,
        [pltpu.VMEM((OCC, NA_D), BF16)],
        2 * OCC * NA_D * HALF,
        "mirror_p" if y_first else "mirror_q",
    )


def direct_kernel(n_in, layout, s_ref, *refs):
    ins, i_ref, keep, send, lhs = refs[:n_in], refs[n_in], refs[-3], refs[-2], refs[-1]
    y_col = s_ref[0]

    @pl.when(pl.program_id(0) == 0)
    def _():
        for source, first, rel_z, rel_y in layout:
            slot = (rel_y ^ y_col) * 2 + rel_z
            rows = pl.ds(pl.multiple_of(slot * 32, 32), 32)
            for k in range(CT):
                tile = pl.multiple_of(s_ref[2 + k] * TILE, TILE)
                lhs[rows, k * TILE : (k + 1) * TILE] = ins[source][
                    first : first + 32, pl.ds(tile, TILE)
                ]

    row = pl.multiple_of(pl.program_id(0) * TN, TN)
    sums = lax.dot_general(
        lhs[...], i_ref[pl.ds(row, TN), :], (((1,), (1,)), ((), ())), preferred_element_type=F32
    )
    keep[0:64] = sums[0:64]
    send[0:64] = sums[64:128]
    keep[64:128] = sums[128:192]
    send[64:128] = sums[192:256]


def direct(scalars, blocks, layout, integrals, name):
    out = (pl.BlockSpec((128, TN), lambda i, s: (0, i)), jax.ShapeDtypeStruct((128, NA_D), F32))
    return call(
        functools.partial(direct_kernel, len(blocks), layout),
        (NA_D // TN,),
        scalars,
        (*blocks, integrals),
        [whole(b.shape) for b in blocks] + [pl.BlockSpec(memory_space=pltpu.VMEM)],
        [out] * 2,
        [pltpu.VMEM((256, NB_D), BF16)],
        2 * 256 * NA_D * NB_D,
        name,
    )


def sum_kernel(n_in, rows, s_ref, *refs):
    ins, outs = refs[:n_in], refs[n_in:]
    for k, o in enumerate(outs):
        part = slice(k * rows, k * rows + rows)
        total = ins[0][part]
        for other in ins[1:]:
            total = total + other[part]
        o[...] = total


def add_split(scalars, parts, rows, name):
    height, width = parts[0].shape
    count = height // rows
    return call(
        functools.partial(sum_kernel, len(parts), rows),
        (width // TN,),
        scalars,
        parts,
        [pl.BlockSpec((height, TN), lambda i, s: (0, i))] * len(parts),
        [(pl.BlockSpec((rows, TN), lambda i, s: (0, i)), jax.ShapeDtypeStruct((rows, width), F32))]
        * count,
        [],
        0,
        name,
    )


def finish_kernel(s_ref, k0, r0, k1, r1, o_ref):
    z_xl = s_ref[1]
    for chunk, (k, r) in enumerate(((k0, r0), (k1, r1))):
        for part in range(4):
            rel = FINISH_Z[chunk][part // 2] * 2 + part % 2
            rows = pl.ds(pl.multiple_of((rel ^ z_xl) * 16, 16), 16)
            own = slice(part * 16, part * 16 + 16)
            o_ref[rows, :] = (k[own] + r[own]).astype(BF16)


FINISH_Z = ((0, 1), (3, 2))


def finish_first(scalars, parts):
    return call(
        finish_kernel,
        (NA_D // TN,),
        scalars,
        parts,
        [pl.BlockSpec((64, TN), lambda i, s: (0, i))] * 4,
        [(pl.BlockSpec((128, TN), lambda i, s: (0, i)), jax.ShapeDtypeStruct((128, NA_D), BF16))],
        [],
        0,
        "finish_first",
    )[0]


def on_device(amp_first, amp_second, integrals, tile_order):
    row, col = lax.axis_index("row"), lax.axis_index("col")
    place = jnp.stack([(row // 8) ^ col, row % 8]).astype(jnp.int32)
    scalars = jnp.concatenate([place, tile_order[0]])

    other = swap(amp_second, xl=1)
    first_core = swap(amp_first, core=1)
    first_xh = swap(amp_first, xh=1)
    block = jnp.concatenate([amp_second, other])
    by_z = [block] + [swap(block, z=r) for r in (1, 2, 3)]
    by_y = [swap(block, y=r) for r in (1, 2, 3)]
    first_both = swap(first_xh, core=1)
    firsts = (amp_first, first_core, first_xh, first_both)
    rest = jnp.concatenate(by_y)
    rest_z = [rest] + [swap(rest, z=r) for r in (1, 2, 3)]

    p = mirror(scalars, firsts, integrals, True, 0)
    q = mirror(scalars, firsts, integrals, False, HALF)
    p = [p[0]] + [swap(p[r], y=r) for r in (1, 2, 3)]
    q = [q[0]] + [swap(q[r], z=r) for r in (1, 2, 3)]
    p = add_split(scalars, p, 32, "sum_p")
    q = add_split(scalars, q, 32, "sum_q")
    p = [p[0]] + [swap(p[r], z=r) for r in (1, 2, 3)]
    q = [q[0]] + [swap(q[r], y=r) for r in (1, 2, 3)]
    p = add_split(scalars, p, 16, "last_p")
    q = add_split(scalars, q, 16, "last_q")
    p = (p[0] + swap(p[1], xl=1)).astype(BF16)
    q = (q[0] + swap(q[1], xl=1)).astype(BF16)
    ladder_second = jnp.concatenate([p, q], axis=1)

    ends = []
    for chunk, zs in enumerate(FINISH_Z):
        blocks, layout = [], []
        for zi, z in enumerate(zs):
            layout.append((len(blocks), 0, zi, 0))
            layout += [(len(blocks) + 1, (y - 1) * 32, zi, y) for y in (1, 2, 3)]
            blocks += [by_z[z], rest_z[z]]
        keep, send = direct(scalars, blocks, layout, integrals, f"direct_{chunk}")
        keep, send = add_split(scalars, (keep, swap(send, core=1)), 64, f"core_{chunk}")
        ends += [keep, swap(send, xh=1)]
    ladder_first = finish_first(scalars, ends)
    return ladder_first, ladder_second


def solution(mesh):
    in_specs = (P("col", "row"), P("row", "col"), P("row", "col"), P("col", None))
    out_specs = (P("col", "row"), P("row", "col"))
    return jax.shard_map(
        on_device, mesh=mesh, in_specs=in_specs, out_specs=out_specs, check_vma=False
    )
```

```python
import functools
import math

import jax
import jax.numpy as jnp
from jax import lax
from jax.experimental import pallas as pl
from jax.experimental.pallas import tpu as pltpu
from jax.sharding import PartitionSpec as P

F32, BF16, I16 = jnp.float32, jnp.bfloat16, jnp.int16
TILE = 256
OCC, NA_D, NB_D, CT = 512, 2048, 4096, 16
TN = 512
P_WIDE = 2560
Q_WIDE = NB_D - P_WIDE
LEVELS = 32766.0
OCTAVE = math.log(2.0) / 16
VMEM_LIMIT = 44 * 2**20
WEIGHT = 0.4


def exchange_pairs(y=0, z=0, xl=0, xh=0, core=0):
    row_flip = y * 8 + z * 2 + xl
    col_flip = xh * 2 + core
    return [
        (row * 4 + col, (row ^ row_flip) * 4 + (col ^ col_flip))
        for row in range(32)
        for col in range(4)
    ]


def swap(what, value, **flips):
    axis, by = next(iter(flips.items()))
    with jax.named_scope(f"{what}_{axis}{by}"):
        return lax.ppermute(value, ("row", "col"), exchange_pairs(**flips))


class Coder:
    def __init__(self, ref):
        self.ref = ref
        self.wide = ref.shape[1] - 128
        self.lane = lax.broadcasted_iota(jnp.int32, (ref.shape[0], 128), 1)
        self.exponents = jnp.zeros((ref.shape[0], 128), jnp.int32)

    def put(self, t, values):
        top = jnp.maximum(jnp.max(jnp.abs(values), axis=1, keepdims=True), 1e-30)
        exponent = jnp.ceil(jnp.log(top) * (1 / OCTAVE) + 0.01)
        inverse = jnp.exp(exponent * -OCTAVE) * LEVELS
        levels = jnp.round(values * inverse).astype(jnp.int32)
        self.ref[:, t * TN : (t + 1) * TN] = levels.astype(I16)
        self.exponents = jnp.where(self.lane == t, exponent.astype(jnp.int32), self.exponents)

    def end(self):
        self.ref[:, self.wide :] = self.exponents.astype(I16)


class Decoder:
    def __init__(self, ref):
        self.ref = ref
        exponents = ref[:, ref.shape[1] - 128 :].astype(jnp.int32).astype(F32)
        self.scales = jnp.exp(exponents * OCTAVE) * (1 / LEVELS)

    def get(self, t, rows=slice(None)):
        levels = self.ref[rows, t * TN : (t + 1) * TN].astype(jnp.int32).astype(F32)
        return levels * self.scales[rows, t : t + 1]


def rows_of(shape):
    return jax.ShapeDtypeStruct(shape, F32)


def coded(rows, wide):
    return jax.ShapeDtypeStruct((rows, wide + 128), I16)


def call(kernel, operands, out_shape, scratch, flops, name, scalars=1, in_hbm=0):
    moved = sum(a.size * a.dtype.itemsize for a in (*operands, *out_shape))
    count = len(operands) - scalars - in_hbm
    return pl.pallas_call(
        kernel,
        in_specs=[pl.BlockSpec(memory_space=pltpu.SMEM)] * scalars
        + [pl.BlockSpec(memory_space=pltpu.VMEM)] * count
        + [pl.BlockSpec(memory_space=pl.ANY)] * in_hbm,
        out_specs=[pl.BlockSpec(memory_space=pltpu.VMEM)] * len(out_shape),
        out_shape=out_shape,
        scratch_shapes=scratch,
        compiler_params=pltpu.CompilerParams(vmem_limit_bytes=VMEM_LIMIT),
        cost_estimate=pl.CostEstimate(
            flops=int(flops * WEIGHT), bytes_accessed=int(moved * WEIGHT), transcendentals=0
        ),
        name=name,
    )(*operands)


def mirror_kernel(xl_first, start, s_ref, f1, f2, f3, f0_ref, i_ref, *refs):
    outs, (lhs, f0, held, sems) = refs[:-4], refs[-4:]
    y_col, z_xl = s_ref[0], s_ref[1]
    height, wide = outs[0].shape
    copies = [
        pltpu.make_async_copy(i_ref.at[:, pl.ds(start + t * TN, TN)], held.at[t], sems.at[t])
        for t in range(wide // TN)
    ]
    copies.append(pltpu.make_async_copy(f0_ref, f0, sems.at[wide // TN]))
    copies[-1].start()
    for copy in copies[:-1]:
        copy.start()
    copies[-1].wait()
    for rel_col, f in enumerate((f0, f1, f2, f3)):
        rel_y = rel_col ^ y_col
        for zx in range(8):
            rel = zx ^ z_xl
            if xl_first:
                slot = (rel & 1) * 16 + rel_y * 4 + (rel >> 1)
            else:
                slot = rel_y * 8 + (rel & 1) * 4 + (rel >> 1)
            lhs[pl.ds(pl.multiple_of(slot * 16, 16), 16), :] = f[zx * 16 : zx * 16 + 16]
    coders = [Coder(o) for o in outs[1:]]
    for t in range(wide // TN):
        copies[t].wait()
        sums = jnp.dot(lhs[...], held[t], preferred_element_type=F32)
        outs[0][:, t * TN : (t + 1) * TN] = sums[:height]
        for k, coder in enumerate(coders):
            coder.put(t, sums[(k + 1) * height : (k + 2) * height])
    for coder in coders:
        coder.end()


def mirror(scalars, firsts, integrals, xl_first, start, wide):
    count = 2 if xl_first else 4
    height = OCC // count
    return call(
        functools.partial(mirror_kernel, xl_first, start),
        (scalars, *firsts[1:], firsts[0], integrals),
        [rows_of((height, wide))] + [coded(height, wide)] * (count - 1),
        [
            pltpu.VMEM((OCC, NA_D), BF16),
            pltpu.VMEM((128, NA_D), BF16),
            pltpu.VMEM((wide // TN, NA_D, TN), BF16),
            pltpu.SemaphoreType.DMA((wide // TN + 1,)),
        ],
        2 * OCC * NA_D * wide,
        "mirror_q" if xl_first else "mirror_p",
        in_hbm=2,
    )


def direct_kernel(s_ref, n0, n1, n2, n3, i_ref, keep, send, lhs, held, sems):
    y_col = s_ref[0]
    copies = [
        pltpu.make_async_copy(i_ref.at[pl.ds(t * TN, TN), :], held.at[t], sems.at[t])
        for t in range(NA_D // TN)
    ]
    for copy in copies:
        copy.start()
    for place, n in enumerate((n0, n1, n2, n3)):
        for rel_y in range(4):
            slot = (rel_y ^ y_col) * 4 + place
            rows = pl.ds(pl.multiple_of(slot * 16, 16), 16)
            for k in range(CT):
                tile = pl.multiple_of(s_ref[2 + k] * TILE, TILE)
                lhs[rows, k * TILE : (k + 1) * TILE] = n[
                    rel_y * 16 : rel_y * 16 + 16, pl.ds(tile, TILE)
                ]
    for t in range(NA_D // TN):
        copies[t].wait()
        columns = slice(t * TN, (t + 1) * TN)
        sums = lax.dot_general(
            lhs[...], held[t], (((1,), (1,)), ((), ())), preferred_element_type=F32
        )
        keep[0:64, columns] = sums[0:64]
        send[0:64, columns] = sums[64:128]
        keep[64:128, columns] = sums[128:192]
        send[64:128, columns] = sums[192:256]


def direct(scalars, blocks, integrals, name):
    return call(
        direct_kernel,
        (scalars, *blocks, integrals),
        [rows_of((128, NA_D))] * 2,
        [
            pltpu.VMEM((256, NB_D), BF16),
            pltpu.VMEM((NA_D // TN, TN, NB_D), BF16),
            pltpu.SemaphoreType.DMA((NA_D // TN,)),
        ],
        2 * 256 * NA_D * NB_D,
        name,
        in_hbm=1,
    )


def fold_kernel(n_in, own, *refs):
    ins, outs = [Decoder(r) for r in refs[:n_in]], refs[n_in:]
    coders = [Coder(o) for o in outs[1:]]
    height = outs[0].shape[0]
    for t in range(own.shape[1] // TN):
        for k in range(len(outs)):
            rows = slice(k * height, k * height + height)
            total = own[rows, t * TN : (t + 1) * TN]
            for other in ins:
                total = total + other.get(t, rows)
            if k == 0:
                outs[0][:, t * TN : (t + 1) * TN] = total
            else:
                coders[k - 1].put(t, total)
    for coder in coders:
        coder.end()


def fold(own, others, count, name):
    height = own.shape[0] // count
    return call(
        functools.partial(fold_kernel, len(others)),
        (own, *others),
        [rows_of((height, own.shape[1]))] + [coded(height, own.shape[1])] * (count - 1),
        [],
        0,
        name,
        scalars=0,
    )


def core_kernel(own, other, keep, send):
    coder = Coder(send)
    for t in range(NA_D // TN):
        columns = slice(t * TN, (t + 1) * TN)
        keep[:, columns] = own[0:64, columns] + other[0:64, columns]
        coder.put(t, own[64:128, columns] + other[64:128, columns])
    coder.end()


def core_fold(own, other, name):
    return call(
        core_kernel, (own, other), [rows_of((64, NA_D)), coded(64, NA_D)], [], 0, name, scalars=0
    )


PARTS = ((0, 1, 2, 6), (3, 7, 4, 5))


def finish_first_kernel(s_ref, k0, r0, k1, r1, o_ref):
    z_xl = s_ref[1]
    for rels, own, other in ((PARTS[0], k0, r0), (PARTS[1], k1, r1)):
        other = Decoder(other)
        for t in range(NA_D // TN):
            columns = slice(t * TN, (t + 1) * TN)
            total = (own[:, columns] + other.get(t)).astype(BF16)
            for part, rel in enumerate(rels):
                rows = pl.ds(pl.multiple_of((rel ^ z_xl) * 16, 16), 16)
                o_ref[rows, columns] = total[part * 16 : part * 16 + 16]


def finish_first(scalars, parts):
    return call(
        finish_first_kernel,
        (scalars, *parts),
        [jax.ShapeDtypeStruct((128, NA_D), BF16)],
        [],
        0,
        "finish_first",
    )[0]


def join_kernel(p, p1, q, q1, q2, q3, keep, *sends):
    coders = [Coder(o) for o in sends]
    for start, own, others in ((0, p, (p1,)), (P_WIDE // TN, q, (q1, q2, q3))):
        others = [Decoder(r) for r in others]
        for t in range(own.shape[1] // TN):
            for k in range(4):
                rows = slice(k * 16, k * 16 + 16)
                total = own[rows, t * TN : (t + 1) * TN]
                for other in others:
                    total = total + other.get(t, rows)
                if k == 0:
                    keep[:, (start + t) * TN : (start + t + 1) * TN] = total
                else:
                    coders[k - 1].put(start + t, total)
    for coder in coders:
        coder.end()


def join(p, q):
    return call(
        join_kernel, (*p, *q), [rows_of((16, NB_D))] + [coded(16, NB_D)] * 3, [], 0, "join", scalars=0
    )


def finish_second_kernel(own, r1, r2, r3, o_ref):
    others = [Decoder(r) for r in (r1, r2, r3)]
    for t in range(NB_D // TN):
        total = own[:, t * TN : (t + 1) * TN]
        for other in others:
            total = total + other.get(t)
        o_ref[:, t * TN : (t + 1) * TN] = total.astype(BF16)


def finish_second(parts):
    return call(
        finish_second_kernel,
        parts,
        [jax.ShapeDtypeStruct((16, NB_D), BF16)],
        [],
        0,
        "finish_second",
        scalars=0,
    )[0]


def together(*values):
    return lax.optimization_barrier(values)


def on_device(amp_first, amp_second, integrals, tile_order):
    row, col = lax.axis_index("row"), lax.axis_index("col")
    place = jnp.stack([(row // 8) ^ col, row % 8]).astype(jnp.int32)
    scalars = jnp.concatenate([place, tile_order[0]])

    first_xh = swap("first", amp_first, xh=1)
    first_core = swap("first", amp_first, core=1)
    y1, y2, y3 = [swap("second", amp_second, y=r) for r in (1, 2, 3)]
    y1, y2, y3, first_xh, first_core = together(y1, y2, y3, first_xh, first_core)
    n0 = jnp.concatenate([amp_second, y1, y2, y3])
    first_both = swap("first", first_xh, core=1)
    firsts = (amp_first, first_core, first_xh, first_both)

    x0 = swap("n", n0, xl=1)
    n1, n3 = swap("n", n0, z=1), swap("n", n0, z=3)
    p = mirror(scalars, firsts, integrals, False, 0, P_WIDE)
    x0, n1, n3, p0, *firsts = together(x0, n1, n3, p[0], *firsts)
    x1, x3 = swap("x", x0, z=1), swap("x", x0, z=3)
    q = mirror(scalars, firsts, integrals, True, P_WIDE, Q_WIDE)
    n3, x1, x3, q0, q1 = together(n3, x1, x3, *q)
    q = (q0, q1)
    n2, x2 = swap("n3", n3, z=1), swap("x1", x1, z=3)

    p1, p3 = swap("p", p[1], y=1), swap("p", p[3], y=3)
    p1, p2, p3 = together(p1, p[2], p3)
    p2 = swap("p", p2, y=2)
    n0, x0, n1, n3 = together(n0, x0, n1, n3, p1)[:4]
    p = fold(p0, [p1, p2, p3], 2, "fold_p_y")
    q = fold(q[0], [swap("q", q[1], xl=1)], 4, "fold_q_xl")
    x1, x3, n2, x2, p0, p1, *q = together(x1, x3, n2, x2, *p, *q)
    p = (p0, p1)
    p_xl = swap("p", p[1], xl=1)
    q1, q2, q3 = [swap("q", q[r], y=r) for r in (1, 2, 3)]
    parts = join((p[0], p_xl), (q[0], q1, q2, q3))
    parts = [parts[0]] + [swap("z", parts[r], z=r) for r in (1, 2, 3)]

    ends = []
    for chunk, blocks in enumerate(((n0, x0, n1, n3), (x1, x3, n2, x2))):
        keep, send = direct(scalars, blocks, integrals, f"direct_{chunk}")
        keep, send = core_fold(keep, swap(f"chunk{chunk}", send, core=1), f"core_{chunk}")
        ends += [keep, swap(f"chunk{chunk}", send, xh=1)]
    ladder_second = finish_second(parts)
    ladder_first = finish_first(scalars, ends)
    return ladder_first, ladder_second


def solution(mesh):
    in_specs = (P("col", "row"), P("row", "col"), P("row", "col"), P("col", None))
    out_specs = (P("col", "row"), P("row", "col"))
    return jax.shard_map(
        on_device, mesh=mesh, in_specs=in_specs, out_specs=out_specs, check_vma=False
    )
```

```python
import functools
import math

import jax
import jax.numpy as jnp
from jax import lax
from jax.experimental import pallas as pl
from jax.experimental.pallas import tpu as pltpu
from jax.sharding import PartitionSpec as P

F32, BF16, I16 = jnp.float32, jnp.bfloat16, jnp.int16
TILE = 256
OCC, NA_D, NB_D, CT = 512, 2048, 4096, 16
TN = 512
CN = 256
P_WIDE = 2560
P_HALF = P_WIDE // 2
Q_WIDE = NB_D - P_WIDE
LEVELS = 32766.0
OCTAVE = math.log(2.0) / 16
VMEM_LIMIT = 16 * 2**20
WEIGHT = 2.5


def exchange_pairs(y=0, z=0, xl=0, xh=0, core=0):
    row_flip = y * 8 + z * 2 + xl
    col_flip = xh * 2 + core
    return [
        (row * 4 + col, (row ^ row_flip) * 4 + (col ^ col_flip))
        for row in range(32)
        for col in range(4)
    ]


def swap(what, value, **flips):
    axis, by = next(iter(flips.items()))
    with jax.named_scope(f"{what}_{axis}{by}"):
        return lax.ppermute(value, ("row", "col"), exchange_pairs(**flips))


class Coder:
    def __init__(self, held, *refs):
        self.held, self.refs = held, refs
        self.lane = lax.broadcasted_iota(jnp.int32, (held.shape[0], 128), 1)
        self.tops = jnp.full((held.shape[0], 128), 1e-30, F32)

    def put(self, t, values):
        self.held[:, t * CN : (t + 1) * CN] = values
        top = jnp.max(jnp.abs(values), axis=1, keepdims=True)
        self.tops = jnp.where(self.lane == t, jnp.maximum(top, 1e-30), self.tops)

    def end(self):
        wide = self.held.shape[1]
        exponents = jnp.ceil(jnp.log(self.tops) * (1 / OCTAVE) + 0.01)
        inverse = jnp.exp(exponents * -OCTAVE) * LEVELS
        exponents = exponents.astype(jnp.int32).astype(I16)
        height = self.refs[0].shape[0]
        for k, ref in enumerate(self.refs):
            rows = slice(k * height, k * height + height)
            ref[:, wide:] = exponents[rows]
            for t in range(wide // CN):
                columns = slice(t * CN, (t + 1) * CN)
                levels = jnp.round(self.held[rows, columns] * inverse[rows, t : t + 1])
                ref[:, columns] = levels.astype(jnp.int32).astype(I16)


def coder_scratch(rows, wide):
    return pltpu.VMEM((rows, wide), F32)


class Decoder:
    def __init__(self, ref):
        self.ref = ref
        exponents = ref[:, ref.shape[1] - 128 :].astype(jnp.int32).astype(F32)
        self.scales = jnp.exp(exponents * OCTAVE) * (1 / LEVELS)

    def get(self, t, rows=slice(None)):
        levels = self.ref[rows, t * CN : (t + 1) * CN].astype(jnp.int32).astype(F32)
        return levels * self.scales[rows, t : t + 1]


def rows_of(shape):
    return jax.ShapeDtypeStruct(shape, F32)


def coded(rows, wide):
    return jax.ShapeDtypeStruct((rows, wide + 128), I16)


def call(kernel, operands, out_shape, scratch, flops, name, scalars=1):
    moved = sum(a.size * a.dtype.itemsize for a in (*operands, *out_shape))
    count = len(operands) - scalars
    return pl.pallas_call(
        kernel,
        in_specs=[pl.BlockSpec(memory_space=pltpu.SMEM)] * scalars
        + [pl.BlockSpec(memory_space=pltpu.VMEM)] * count,
        out_specs=[pl.BlockSpec(memory_space=pltpu.VMEM)] * len(out_shape),
        out_shape=out_shape,
        scratch_shapes=scratch,
        compiler_params=pltpu.CompilerParams(vmem_limit_bytes=VMEM_LIMIT),
        cost_estimate=pl.CostEstimate(
            flops=int(flops * WEIGHT), bytes_accessed=int(moved * WEIGHT), transcendentals=0
        ),
        name=name,
    )(*operands)


def product_lhs(z_xl, blocks, lhs):
    for k, f in enumerate(blocks):
        for zx in range(8):
            rel = zx ^ z_xl
            slot = k * 8 + (rel & 1) * 4 + (rel >> 1)
            lhs[pl.ds(pl.multiple_of(slot * 16, 16), 16), :] = f[zx * 16 : zx * 16 + 16]


def early_kernel(start, s_ref, f0, f1, i_ref, out, lhs):
    product_lhs(s_ref[1], (f0, f1), lhs)
    for t in range(out.shape[1] // TN):
        columns = slice(start + t * TN, start + (t + 1) * TN)
        sums = jnp.dot(lhs[...], i_ref[:, columns], preferred_element_type=F32)
        out[:, t * TN : (t + 1) * TN] = sums


def early(scalars, firsts, integrals, start, wide, name):
    return call(
        functools.partial(early_kernel, start),
        (scalars, *firsts, integrals),
        [rows_of((256, wide))],
        [pltpu.VMEM((256, NA_D), BF16)],
        2 * 256 * NA_D * wide,
        name,
    )[0]


def mirror_p_kernel(
    s_ref,
    f2,
    f3,
    early_ref,
    i_ref,
    keep_a,
    send_a,
    keep_b,
    send_b,
    lhs,
    sums,
    held_a,
    held_b,
):
    y_col = s_ref[0]
    product_lhs(s_ref[1], (f2, f3), lhs)
    coders = [Coder(held_a, send_a), Coder(held_b, send_b)]
    for t in range(P_WIDE // TN):
        columns = slice(t * TN, (t + 1) * TN)
        late = jnp.dot(lhs[...], i_ref[:, columns], preferred_element_type=F32)
        for k in range(2):
            rows = slice(k * 128, k * 128 + 128)
            sums[pl.ds(pl.multiple_of((k ^ y_col) * 128, 128), 128), :] = early_ref[rows, columns]
            sums[pl.ds(pl.multiple_of(((k + 2) ^ y_col) * 128, 128), 128), :] = late[rows]
        for part in range(TN // CN):
            half, tile = divmod(t * (TN // CN) + part, P_HALF // CN)
            y0, y1, y2, y3 = [
                sums[y * 128 : y * 128 + 128, part * CN : part * CN + CN] for y in range(4)
            ]
            place = slice(tile * CN, tile * CN + CN)
            if half == 0:
                keep_a[0:128, place], keep_a[128:256, place] = y0, y1
                coders[0].put(tile, jnp.concatenate([y3, y2]))
            else:
                keep_b[0:128, place], keep_b[128:256, place] = y0, y3
                coders[1].put(tile, jnp.concatenate([y1, y2]))
    for coder in coders:
        coder.end()


def mirror_p(scalars, firsts, first_sums, integrals):
    return call(
        mirror_p_kernel,
        (scalars, *firsts, first_sums, integrals),
        [rows_of((256, P_HALF)), coded(256, P_HALF)] * 2,
        [pltpu.VMEM((256, NA_D), BF16), pltpu.VMEM((OCC, TN), F32)]
        + [coder_scratch(256, P_HALF)] * 2,
        2 * 256 * NA_D * P_WIDE,
        "mirror_p",
    )


def mirror_q_kernel(s_ref, f2, f3, early_ref, i_ref, keep, send, lhs, sums, coding):
    y_col = s_ref[0]
    product_lhs(s_ref[1], (f2, f3), lhs)
    coder = Coder(coding, send)
    for t in range(Q_WIDE // TN):
        columns = slice(P_WIDE + t * TN, P_WIDE + (t + 1) * TN)
        late = jnp.dot(lhs[...], i_ref[:, columns], preferred_element_type=F32)
        for k in range(4):
            for xl in range(2):
                rows = slice((k % 2) * 128 + xl * 64, (k % 2) * 128 + xl * 64 + 64)
                place = pl.ds(pl.multiple_of(xl * 256 + (k ^ y_col) * 64, 64), 64)
                sums[place, :] = early_ref[rows, t * TN : (t + 1) * TN] if k < 2 else late[rows]
        keep[:, t * TN : (t + 1) * TN] = sums[0:256]
        for part in range(TN // CN):
            coder.put(t * (TN // CN) + part, sums[256:512, part * CN : part * CN + CN])
    coder.end()


def mirror_q(scalars, firsts, first_sums, integrals):
    return call(
        mirror_q_kernel,
        (scalars, *firsts, first_sums, integrals),
        [rows_of((256, Q_WIDE)), coded(256, Q_WIDE)],
        [
            pltpu.VMEM((256, NA_D), BF16),
            pltpu.VMEM((OCC, TN), F32),
            coder_scratch(256, Q_WIDE),
        ],
        2 * 256 * NA_D * Q_WIDE,
        "mirror_q",
    )


def direct_kernel(s_ref, n0, n1, n2, n3, i_ref, keep, send, lhs):
    y_col = s_ref[0]
    for place, n in enumerate((n0, n1, n2, n3)):
        for rel_y in range(4):
            slot = (rel_y ^ y_col) * 4 + place
            rows = pl.ds(pl.multiple_of(slot * 16, 16), 16)
            for k in range(CT):
                tile = pl.multiple_of(s_ref[2 + k] * TILE, TILE)
                lhs[rows, k * TILE : (k + 1) * TILE] = n[
                    rel_y * 16 : rel_y * 16 + 16, pl.ds(tile, TILE)
                ]
    for t in range(NA_D // TN):
        columns = slice(t * TN, (t + 1) * TN)
        sums = lax.dot_general(
            lhs[...], i_ref[columns, :], (((1,), (1,)), ((), ())), preferred_element_type=F32
        )
        keep[0:64, columns] = sums[0:64]
        send[0:64, columns] = sums[64:128]
        keep[64:128, columns] = sums[128:192]
        send[64:128, columns] = sums[192:256]


def direct(scalars, blocks, integrals, name):
    return call(
        direct_kernel,
        (scalars, *blocks, integrals),
        [rows_of((128, NA_D))] * 2,
        [pltpu.VMEM((256, NB_D), BF16)],
        2 * 256 * NA_D * NB_D,
        name,
    )


def fold_kernel(own, other, keep, *refs):
    sends, held = refs[:-1], refs[-1]
    other, coder = Decoder(other), Coder(held, *sends)
    height = keep.shape[0]
    for t in range(own.shape[1] // CN):
        total = own[:, t * CN : (t + 1) * CN] + other.get(t)
        keep[:, t * CN : (t + 1) * CN] = total[:height]
        coder.put(t, total[height:])
    coder.end()


def fold(own, other, count, name):
    rows, wide = own.shape
    height = rows // count
    return call(
        fold_kernel,
        (own, other),
        [rows_of((height, wide))] + [coded(height, wide)] * (count - 1),
        [coder_scratch(rows - height, wide)],
        0,
        name,
        scalars=0,
    )


def merge_kernel(a, a1, b, b1, keep, send, held):
    coder = Coder(held, send)
    for half, (own, other) in enumerate(((a, Decoder(a1)), (b, Decoder(b1)))):
        for t in range(P_HALF // CN):
            tile = half * (P_HALF // CN) + t
            total = own[:, t * CN : (t + 1) * CN] + other.get(t)
            keep[:, tile * CN : (tile + 1) * CN] = total[0:64]
            coder.put(tile, total[64:128])
    coder.end()


def merge(parts):
    return call(
        merge_kernel,
        parts,
        [rows_of((64, P_WIDE)), coded(64, P_WIDE)],
        [coder_scratch(64, P_WIDE)],
        0,
        "merge",
        scalars=0,
    )


def core_kernel(own, other, keep, send, held):
    coder = Coder(held, send)
    for t in range(NA_D // CN):
        columns = slice(t * CN, (t + 1) * CN)
        keep[:, columns] = own[0:64, columns] + other[0:64, columns]
        coder.put(t, own[64:128, columns] + other[64:128, columns])
    coder.end()


def core_fold(own, other, name):
    return call(
        core_kernel,
        (own, other),
        [rows_of((64, NA_D)), coded(64, NA_D)],
        [coder_scratch(64, NA_D)],
        0,
        name,
        scalars=0,
    )


PARTS = ((0, 1, 2, 6), (3, 7, 4, 5))


def finish_first_kernel(s_ref, k0, r0, k1, r1, o_ref):
    z_xl = s_ref[1]
    for rels, own, other in ((PARTS[0], k0, r0), (PARTS[1], k1, r1)):
        other = Decoder(other)
        for t in range(NA_D // CN):
            columns = slice(t * CN, (t + 1) * CN)
            total = (own[:, columns] + other.get(t)).astype(BF16)
            for part, rel in enumerate(rels):
                rows = pl.ds(pl.multiple_of((rel ^ z_xl) * 16, 16), 16)
                o_ref[rows, columns] = total[part * 16 : part * 16 + 16]


def finish_first(scalars, parts):
    return call(
        finish_first_kernel,
        (scalars, *parts),
        [jax.ShapeDtypeStruct((128, NA_D), BF16)],
        [],
        0,
        "finish_first",
    )[0]


def join_kernel(p, p1, q, q1, q2, q3, keep, send1, send2, send3, held):
    coder = Coder(held, send1, send2, send3)
    for start, own, others in ((0, p, (p1,)), (P_WIDE // CN, q, (q1, q2, q3))):
        others = [Decoder(r) for r in others]
        for t in range(own.shape[1] // CN):
            total = own[:, t * CN : (t + 1) * CN]
            for other in others:
                total = total + other.get(t)
            keep[:, (start + t) * CN : (start + t + 1) * CN] = total[0:16]
            coder.put(start + t, total[16:64])
    coder.end()


def join(p, q):
    return call(
        join_kernel,
        (*p, *q),
        [rows_of((16, NB_D))] + [coded(16, NB_D)] * 3,
        [coder_scratch(48, NB_D)],
        0,
        "join",
        scalars=0,
    )


def finish_second_kernel(own, r1, r2, r3, o_ref):
    others = [Decoder(r) for r in (r1, r2, r3)]
    for t in range(NB_D // CN):
        total = own[:, t * CN : (t + 1) * CN]
        for other in others:
            total = total + other.get(t)
        o_ref[:, t * CN : (t + 1) * CN] = total.astype(BF16)


def finish_second(parts):
    return call(
        finish_second_kernel,
        parts,
        [jax.ShapeDtypeStruct((16, NB_D), BF16)],
        [],
        0,
        "finish_second",
        scalars=0,
    )[0]


def together(*values):
    return lax.optimization_barrier(values)


def on_device(amp_first, amp_second, integrals, tile_order):
    row, col = lax.axis_index("row"), lax.axis_index("col")
    place = jnp.stack([(row // 8) ^ col, row % 8]).astype(jnp.int32)
    scalars = jnp.concatenate([place, tile_order[0]])

    second = amp_second
    first_xh = swap("first", amp_first, xh=1)
    first_core = swap("first", amp_first, core=1)
    y1, y2, y3 = [swap("second", second, y=r) for r in (1, 2, 3)]
    sums_p = early(scalars, (amp_first, first_core), integrals, 0, P_WIDE, "early_p")
    sums_q = early(scalars, (amp_first, first_core), integrals, P_WIDE, Q_WIDE, "early_q")
    y1, y2, y3, scalars, first_xh, sums_p, sums_q = together(y1, y2, y3, scalars, first_xh, sums_p, sums_q)
    n0 = jnp.concatenate([second, y1, y2, y3])
    first_both = swap("first", first_xh, core=1)
    x0 = swap("n", n0, xl=1)
    n1, n3 = swap("n", n0, z=1), swap("n", n0, z=3)
    pa, pa_send, pb, pb_send = mirror_p(scalars, (first_xh, first_both), sums_p, integrals)
    pa_got, pb_got = swap("pa", pa_send, y=3), swap("pb", pb_send, y=1)
    pa, pb, sums_q, first_xh, first_both = together(pa, pb, sums_q, first_xh, first_both)
    q, q_send = mirror_q(scalars, (first_xh, first_both), sums_q, integrals)
    n0, x0, n1, n3, q, q_send = together(n0, x0, n1, n3, q, q_send)
    q_got = swap("q", q_send, xl=1)
    x1, x3 = swap("x", x0, z=1), swap("x", x0, z=3)
    keep0, send0 = direct(scalars, (n0, x0, n1, n3), integrals, "direct_0")
    pa, pa_got, pb, pb_got = together(pa, pa_got, pb, pb_got)
    pa, pa_send = fold(pa, pa_got, 2, "fold_pa")
    pb, pb_send = fold(pb, pb_got, 2, "fold_pb")
    pa_got, pb_got = swap("pa", pa_send, y=1), swap("pb", pb_send, y=3)
    got0 = swap("chunk0", send0, core=1)
    n3, x1, x3, pa, pb = together(n3, x1, x3, pa, pb)
    q = fold(q, q_got, 4, "fold_q_xl")
    n2, x2 = swap("n3", n3, z=1), swap("x1", x1, z=3)
    p, p_send = merge((pa, pa_got, pb, pb_got))
    p, p_send, *q = together(p, p_send, *q)
    p_got = swap("p", p_send, xl=1)
    q_got = [swap("q", q[r], y=r) for r in (1, 2, 3)]
    keep0, send0 = core_fold(keep0, got0, "core_0")
    got0 = swap("chunk0", send0, xh=1)
    x1, x3, n2, x2, p = together(x1, x3, n2, x2, p)
    keep1, send1 = direct(scalars, (x1, x3, n2, x2), integrals, "direct_1")
    p_got, keep1, send1, *q_got = together(p_got, keep1, send1, *q_got)
    parts = join((p, p_got), (q[0], *q_got))
    got1 = swap("chunk1", send1, core=1)
    keep1, got1, *parts = together(keep1, got1, *parts)
    parts = [parts[0]] + [swap("z", parts[r], z=r) for r in (1, 2, 3)]
    keep1, send1 = core_fold(keep1, got1, "core_1")
    got1 = swap("chunk1", send1, xh=1)
    ladder_first = finish_first(scalars, (keep0, got0, keep1, got1))
    ladder_first, *parts = together(ladder_first, *parts)
    ladder_second = finish_second(parts)
    return ladder_first, ladder_second


def solution(mesh):
    in_specs = (P("col", "row"), P("row", "col"), P("row", "col"), P("col", None))
    out_specs = (P("col", "row"), P("row", "col"))
    return jax.shard_map(
        on_device, mesh=mesh, in_specs=in_specs, out_specs=out_specs, check_vma=False
    )
```

```python
import functools
import math

import jax
import jax.numpy as jnp
from jax import lax
from jax.experimental import pallas as pl
from jax.experimental.pallas import tpu as pltpu
from jax.sharding import PartitionSpec as P

F32, BF16, I16 = jnp.float32, jnp.bfloat16, jnp.int16
TILE = 256
OCC, NA_D, NB_D, CT = 512, 2048, 4096, 16
TN = 512
CN = 512
P_WIDE = 3072
P_HALF = P_WIDE // 2
Q_WIDE = NB_D - P_WIDE
LEVELS = 32766.0
OCTAVE = math.log(2.0) / 16
VMEM_LIMIT = 16 * 2**20
WEIGHT = 2.5


def exchange_pairs(y=0, z=0, xl=0, xh=0, core=0):
    row_flip = y * 8 + z * 2 + xl
    col_flip = xh * 2 + core
    return [
        (row * 4 + col, (row ^ row_flip) * 4 + (col ^ col_flip))
        for row in range(32)
        for col in range(4)
    ]


def swap(what, value, **flips):
    axis, by = next(iter(flips.items()))
    with jax.named_scope(f"{what}_{axis}{by}"):
        return lax.ppermute(value, ("row", "col"), exchange_pairs(**flips))


class Coder:
    def __init__(self, held, *refs):
        self.held, self.refs = held, refs
        self.lane = lax.broadcasted_iota(jnp.int32, (held.shape[0], 128), 1)
        self.tops = jnp.full((held.shape[0], 128), 1e-30, F32)

    def put(self, t, values):
        self.held[:, t * CN : (t + 1) * CN] = values
        top = jnp.max(jnp.abs(values), axis=1, keepdims=True)
        self.tops = jnp.where(self.lane == t, jnp.maximum(top, 1e-30), self.tops)

    def end(self):
        wide = self.held.shape[1]
        exponents = jnp.ceil(jnp.log(self.tops) * (1 / OCTAVE) + 0.01)
        inverse = jnp.exp(exponents * -OCTAVE) * LEVELS
        exponents = exponents.astype(jnp.int32).astype(I16)
        height = self.refs[0].shape[0]
        for k, ref in enumerate(self.refs):
            rows = slice(k * height, k * height + height)
            ref[:, wide:] = exponents[rows]
            for t in range(wide // CN):
                columns = slice(t * CN, (t + 1) * CN)
                levels = jnp.round(self.held[rows, columns] * inverse[rows, t : t + 1])
                ref[:, columns] = levels.astype(jnp.int32).astype(I16)


def coder_scratch(rows, wide):
    return pltpu.VMEM((rows, wide), F32)


class Decoder:
    def __init__(self, ref):
        self.ref = ref
        exponents = ref[:, ref.shape[1] - 128 :].astype(jnp.int32).astype(F32)
        self.scales = jnp.exp(exponents * OCTAVE) * (1 / LEVELS)

    def get(self, t, rows=slice(None)):
        levels = self.ref[rows, t * CN : (t + 1) * CN].astype(jnp.int32).astype(F32)
        return levels * self.scales[rows, t : t + 1]


def rows_of(shape):
    return jax.ShapeDtypeStruct(shape, F32)


def coded(rows, wide):
    return jax.ShapeDtypeStruct((rows, wide + 128), I16)


def call(kernel, operands, out_shape, scratch, flops, name, scalars=1):
    moved = sum(a.size * a.dtype.itemsize for a in (*operands, *out_shape))
    count = len(operands) - scalars
    return pl.pallas_call(
        kernel,
        in_specs=[pl.BlockSpec(memory_space=pltpu.SMEM)] * scalars
        + [pl.BlockSpec(memory_space=pltpu.VMEM)] * count,
        out_specs=[pl.BlockSpec(memory_space=pltpu.VMEM)] * len(out_shape),
        out_shape=out_shape,
        scratch_shapes=scratch,
        compiler_params=pltpu.CompilerParams(vmem_limit_bytes=VMEM_LIMIT),
        cost_estimate=pl.CostEstimate(
            flops=int(flops * WEIGHT), bytes_accessed=int(moved * WEIGHT), transcendentals=0
        ),
        name=name,
    )(*operands)


def product_lhs(z_xl, blocks, lhs):
    for k, f in enumerate(blocks):
        for zx in range(8):
            rel = zx ^ z_xl
            slot = k * 8 + (rel & 1) * 4 + (rel >> 1)
            lhs[pl.ds(pl.multiple_of(slot * 16, 16), 16), :] = f[zx * 16 : zx * 16 + 16]


def early_kernel(start, s_ref, f0, f1, i_ref, out, lhs):
    product_lhs(s_ref[1], (f0, f1), lhs)
    for t in range(out.shape[1] // TN):
        columns = slice(start + t * TN, start + (t + 1) * TN)
        sums = jnp.dot(lhs[...], i_ref[:, columns], preferred_element_type=F32)
        out[:, t * TN : (t + 1) * TN] = sums


def early(scalars, firsts, integrals, start, wide, name):
    return call(
        functools.partial(early_kernel, start),
        (scalars, *firsts, integrals),
        [rows_of((256, wide))],
        [pltpu.VMEM((256, NA_D), BF16)],
        2 * 256 * NA_D * wide,
        name,
    )[0]


def mirror_p_kernel(
    s_ref,
    f2,
    f3,
    early_ref,
    i_ref,
    keep_a,
    send_a,
    keep_b,
    send_b,
    lhs,
    sums,
    held_a,
    held_b,
):
    y_col = s_ref[0]
    product_lhs(s_ref[1], (f2, f3), lhs)
    coders = [Coder(held_a, send_a), Coder(held_b, send_b)]
    for t in range(P_WIDE // TN):
        columns = slice(t * TN, (t + 1) * TN)
        late = jnp.dot(lhs[...], i_ref[:, columns], preferred_element_type=F32)
        for k in range(2):
            rows = slice(k * 128, k * 128 + 128)
            sums[pl.ds(pl.multiple_of((k ^ y_col) * 128, 128), 128), :] = early_ref[rows, columns]
            sums[pl.ds(pl.multiple_of(((k + 2) ^ y_col) * 128, 128), 128), :] = late[rows]
        for part in range(TN // CN):
            half, tile = divmod(t * (TN // CN) + part, P_HALF // CN)
            y0, y1, y2, y3 = [
                sums[y * 128 : y * 128 + 128, part * CN : part * CN + CN] for y in range(4)
            ]
            place = slice(tile * CN, tile * CN + CN)
            if half == 0:
                keep_a[0:128, place], keep_a[128:256, place] = y0, y1
                coders[0].put(tile, jnp.concatenate([y3, y2]))
            else:
                keep_b[0:128, place], keep_b[128:256, place] = y0, y3
                coders[1].put(tile, jnp.concatenate([y1, y2]))
    for coder in coders:
        coder.end()


def mirror_p(scalars, firsts, first_sums, integrals):
    return call(
        mirror_p_kernel,
        (scalars, *firsts, first_sums, integrals),
        [rows_of((256, P_HALF)), coded(256, P_HALF)] * 2,
        [pltpu.VMEM((256, NA_D), BF16), pltpu.VMEM((OCC, TN), F32)]
        + [coder_scratch(256, P_HALF)] * 2,
        2 * 256 * NA_D * P_WIDE,
        "mirror_p",
    )


def mirror_q_kernel(s_ref, f2, f3, early_ref, i_ref, keep, send, lhs, sums, coding):
    y_col = s_ref[0]
    product_lhs(s_ref[1], (f2, f3), lhs)
    coder = Coder(coding, send)
    for t in range(Q_WIDE // TN):
        columns = slice(P_WIDE + t * TN, P_WIDE + (t + 1) * TN)
        late = jnp.dot(lhs[...], i_ref[:, columns], preferred_element_type=F32)
        for k in range(4):
            for xl in range(2):
                rows = slice((k % 2) * 128 + xl * 64, (k % 2) * 128 + xl * 64 + 64)
                place = pl.ds(pl.multiple_of(xl * 256 + (k ^ y_col) * 64, 64), 64)
                sums[place, :] = early_ref[rows, t * TN : (t + 1) * TN] if k < 2 else late[rows]
        keep[:, t * TN : (t + 1) * TN] = sums[0:256]
        for part in range(TN // CN):
            coder.put(t * (TN // CN) + part, sums[256:512, part * CN : part * CN + CN])
    coder.end()


def mirror_q(scalars, firsts, first_sums, integrals):
    return call(
        mirror_q_kernel,
        (scalars, *firsts, first_sums, integrals),
        [rows_of((256, Q_WIDE)), coded(256, Q_WIDE)],
        [
            pltpu.VMEM((256, NA_D), BF16),
            pltpu.VMEM((OCC, TN), F32),
            coder_scratch(256, Q_WIDE),
        ],
        2 * 256 * NA_D * Q_WIDE,
        "mirror_q",
    )


def direct_kernel(s_ref, n0, n1, n2, n3, i_ref, keep, send, lhs):
    y_col = s_ref[0]
    for place, n in enumerate((n0, n1, n2, n3)):
        for rel_y in range(4):
            slot = (rel_y ^ y_col) * 4 + place
            rows = pl.ds(pl.multiple_of(slot * 16, 16), 16)
            for k in range(CT):
                tile = pl.multiple_of(s_ref[2 + k] * TILE, TILE)
                lhs[rows, k * TILE : (k + 1) * TILE] = n[
                    rel_y * 16 : rel_y * 16 + 16, pl.ds(tile, TILE)
                ]
    for t in range(NA_D // TN):
        columns = slice(t * TN, (t + 1) * TN)
        sums = lax.dot_general(
            lhs[...], i_ref[columns, :], (((1,), (1,)), ((), ())), preferred_element_type=F32
        )
        keep[0:64, columns] = sums[0:64]
        send[0:64, columns] = sums[64:128]
        keep[64:128, columns] = sums[128:192]
        send[64:128, columns] = sums[192:256]


def direct(scalars, blocks, integrals, name):
    return call(
        direct_kernel,
        (scalars, *blocks, integrals),
        [rows_of((128, NA_D))] * 2,
        [pltpu.VMEM((256, NB_D), BF16)],
        2 * 256 * NA_D * NB_D,
        name,
    )


def fold_kernel(own, other, keep, *refs):
    sends, held = refs[:-1], refs[-1]
    other, coder = Decoder(other), Coder(held, *sends)
    height = keep.shape[0]
    for t in range(own.shape[1] // CN):
        total = own[:, t * CN : (t + 1) * CN] + other.get(t)
        keep[:, t * CN : (t + 1) * CN] = total[:height]
        coder.put(t, total[height:])
    coder.end()


def fold(own, other, count, name):
    rows, wide = own.shape
    height = rows // count
    return call(
        fold_kernel,
        (own, other),
        [rows_of((height, wide))] + [coded(height, wide)] * (count - 1),
        [coder_scratch(rows - height, wide)],
        0,
        name,
        scalars=0,
    )


def merge_kernel(a, a1, b, b1, keep, send, held):
    coder = Coder(held, send)
    for half, (own, other) in enumerate(((a, Decoder(a1)), (b, Decoder(b1)))):
        for t in range(P_HALF // CN):
            tile = half * (P_HALF // CN) + t
            total = own[:, t * CN : (t + 1) * CN] + other.get(t)
            keep[:, tile * CN : (tile + 1) * CN] = total[0:64]
            coder.put(tile, total[64:128])
    coder.end()


def merge(parts):
    return call(
        merge_kernel,
        parts,
        [rows_of((64, P_WIDE)), coded(64, P_WIDE)],
        [coder_scratch(64, P_WIDE)],
        0,
        "merge",
        scalars=0,
    )


def core_kernel(own, other, keep, send, held):
    coder = Coder(held, send)
    for t in range(NA_D // CN):
        columns = slice(t * CN, (t + 1) * CN)
        keep[:, columns] = own[0:64, columns] + other[0:64, columns]
        coder.put(t, own[64:128, columns] + other[64:128, columns])
    coder.end()


def core_fold(own, other, name):
    return call(
        core_kernel,
        (own, other),
        [rows_of((64, NA_D)), coded(64, NA_D)],
        [coder_scratch(64, NA_D)],
        0,
        name,
        scalars=0,
    )


PARTS = ((0, 1, 2, 6), (3, 7, 4, 5))


def finish_first_kernel(s_ref, k0, r0, k1, r1, o_ref):
    z_xl = s_ref[1]
    for rels, own, other in ((PARTS[0], k0, r0), (PARTS[1], k1, r1)):
        other = Decoder(other)
        for t in range(NA_D // CN):
            columns = slice(t * CN, (t + 1) * CN)
            total = (own[:, columns] + other.get(t)).astype(BF16)
            for part, rel in enumerate(rels):
                rows = pl.ds(pl.multiple_of((rel ^ z_xl) * 16, 16), 16)
                o_ref[rows, columns] = total[part * 16 : part * 16 + 16]


def finish_first(scalars, parts):
    return call(
        finish_first_kernel,
        (scalars, *parts),
        [jax.ShapeDtypeStruct((128, NA_D), BF16)],
        [],
        0,
        "finish_first",
    )[0]


def join_kernel(p, p1, q, q1, q2, q3, keep, send1, send2, send3, held):
    coder = Coder(held, send1, send2, send3)
    for start, own, others in ((0, p, (p1,)), (P_WIDE // CN, q, (q1, q2, q3))):
        others = [Decoder(r) for r in others]
        for t in range(own.shape[1] // CN):
            total = own[:, t * CN : (t + 1) * CN]
            for other in others:
                total = total + other.get(t)
            keep[:, (start + t) * CN : (start + t + 1) * CN] = total[0:16]
            coder.put(start + t, total[16:64])
    coder.end()


def join(p, q):
    return call(
        join_kernel,
        (*p, *q),
        [rows_of((16, NB_D))] + [coded(16, NB_D)] * 3,
        [coder_scratch(48, NB_D)],
        0,
        "join",
        scalars=0,
    )


def finish_second_kernel(own, r1, r2, r3, o_ref):
    others = [Decoder(r) for r in (r1, r2, r3)]
    for t in range(NB_D // CN):
        total = own[:, t * CN : (t + 1) * CN]
        for other in others:
            total = total + other.get(t)
        o_ref[:, t * CN : (t + 1) * CN] = total.astype(BF16)


def finish_second(parts):
    return call(
        finish_second_kernel,
        parts,
        [jax.ShapeDtypeStruct((16, NB_D), BF16)],
        [],
        0,
        "finish_second",
        scalars=0,
    )[0]


def together(*values):
    return lax.optimization_barrier(values)


def on_device(amp_first, amp_second, integrals, tile_order):
    row, col = lax.axis_index("row"), lax.axis_index("col")
    place = jnp.stack([(row // 8) ^ col, row % 8]).astype(jnp.int32)
    scalars = jnp.concatenate([place, tile_order[0]])

    second = amp_second
    first_xh = swap("first", amp_first, xh=1)
    first_core = swap("first", amp_first, core=1)
    y1, y2, y3 = [swap("second", second, y=r) for r in (1, 2, 3)]
    sums_p = early(scalars, (amp_first, first_core), integrals, 0, P_WIDE, "early_p")
    sums_q = early(scalars, (amp_first, first_core), integrals, P_WIDE, Q_WIDE, "early_q")
    y1, y2, y3, scalars, sums_p = together(y1, y2, y3, scalars, sums_p)
    n0 = jnp.concatenate([second, y1, y2, y3])
    first_both = swap("first", first_xh, core=1)
    x0 = swap("n", n0, xl=1)
    n1, n3 = swap("n", n0, z=1), swap("n", n0, z=3)
    pa, pa_send, pb, pb_send = mirror_p(scalars, (first_xh, first_both), sums_p, integrals)
    pa_got, pb_got = swap("pa", pa_send, y=3), swap("pb", pb_send, y=1)
    pa, pb, sums_q, first_xh, first_both = together(pa, pb, sums_q, first_xh, first_both)
    q, q_send = mirror_q(scalars, (first_xh, first_both), sums_q, integrals)
    n0, x0, n1, n3, q, q_send = together(n0, x0, n1, n3, q, q_send)
    q_got = swap("q", q_send, xl=1)
    x1, x3 = swap("x", x0, z=1), swap("x", x0, z=3)
    keep0, send0 = direct(scalars, (n0, x0, n1, n3), integrals, "direct_0")
    pa, pa_got, pb, pb_got = together(pa, pa_got, pb, pb_got)
    pa, pa_send = fold(pa, pa_got, 2, "fold_pa")
    pb, pb_send = fold(pb, pb_got, 2, "fold_pb")
    pa_got, pb_got = swap("pa", pa_send, y=1), swap("pb", pb_send, y=3)
    got0 = swap("chunk0", send0, core=1)
    n3, x1, x3, pa, pb = together(n3, x1, x3, pa, pb)
    q = fold(q, q_got, 4, "fold_q_xl")
    n2, x2 = swap("n3", n3, z=1), swap("x1", x1, z=3)
    p, p_send = merge((pa, pa_got, pb, pb_got))
    p, p_send, *q = together(p, p_send, *q)
    p_got = swap("p", p_send, xl=1)
    q_got = [swap("q", q[r], y=r) for r in (1, 2, 3)]
    keep0, send0 = core_fold(keep0, got0, "core_0")
    got0 = swap("chunk0", send0, xh=1)
    x1, x3, n2, x2, p = together(x1, x3, n2, x2, p)
    keep1, send1 = direct(scalars, (x1, x3, n2, x2), integrals, "direct_1")
    p_got, keep1, send1, *q_got = together(p_got, keep1, send1, *q_got)
    parts = join((p, p_got), (q[0], *q_got))
    got1 = swap("chunk1", send1, core=1)
    keep1, got1, *parts = together(keep1, got1, *parts)
    parts = [parts[0]] + [swap("z", parts[r], z=r) for r in (1, 2, 3)]
    keep1, send1 = core_fold(keep1, got1, "core_1")
    got1 = swap("chunk1", send1, xh=1)
    ladder_first = finish_first(scalars, (keep0, got0, keep1, got1))
    ladder_first, *parts = together(ladder_first, *parts)
    ladder_second = finish_second(parts)
    return ladder_first, ladder_second


def solution(mesh):
    in_specs = (P("col", "row"), P("row", "col"), P("row", "col"), P("col", None))
    out_specs = (P("col", "row"), P("row", "col"))
    return jax.shard_map(
        on_device, mesh=mesh, in_specs=in_specs, out_specs=out_specs, check_vma=False
    )
```

```python
import functools
import math

import jax
import jax.numpy as jnp
from jax import lax
from jax.experimental import pallas as pl
from jax.experimental.pallas import tpu as pltpu
from jax.sharding import PartitionSpec as P

F32, BF16, I16 = jnp.float32, jnp.bfloat16, jnp.int16
TILE = 256
OCC, NA_D, NB_D, CT = 512, 2048, 4096, 16
TN = 1024
CN = 512
P_WIDE = 3072
P_HALF = P_WIDE // 2
Q_WIDE = NB_D - P_WIDE
LEVELS = 32766.0
OCTAVE = math.log(2.0) / 16
VMEM_LIMIT = 16 * 2**20
WEIGHT = 2.5


def exchange_pairs(y=0, z=0, xl=0, xh=0, core=0):
    row_flip = y * 8 + z * 2 + xl
    col_flip = xh * 2 + core
    return [
        (row * 4 + col, (row ^ row_flip) * 4 + (col ^ col_flip))
        for row in range(32)
        for col in range(4)
    ]


def swap(what, value, **flips):
    axis, by = next(iter(flips.items()))
    with jax.named_scope(f"{what}_{axis}{by}"):
        return lax.ppermute(value, ("row", "col"), exchange_pairs(**flips))


class Coder:
    def __init__(self, held, *refs):
        self.held, self.refs = held, refs
        self.lane = lax.broadcasted_iota(jnp.int32, (held.shape[0], 128), 1)
        self.tops = jnp.full((held.shape[0], 128), 1e-30, F32)

    def put(self, t, values):
        self.held[:, t * CN : (t + 1) * CN] = values
        top = jnp.max(jnp.abs(values), axis=1, keepdims=True)
        self.tops = jnp.where(self.lane == t, jnp.maximum(top, 1e-30), self.tops)

    def end(self):
        wide = self.held.shape[1]
        exponents = jnp.ceil(jnp.log(self.tops) * (1 / OCTAVE) + 0.01)
        inverse = jnp.exp(exponents * -OCTAVE) * LEVELS
        exponents = exponents.astype(jnp.int32).astype(I16)
        height = self.refs[0].shape[0]
        for k, ref in enumerate(self.refs):
            rows = slice(k * height, k * height + height)
            ref[:, wide:] = exponents[rows]
            for t in range(wide // CN):
                columns = slice(t * CN, (t + 1) * CN)
                levels = jnp.round(self.held[rows, columns] * inverse[rows, t : t + 1])
                ref[:, columns] = levels.astype(jnp.int32).astype(I16)


def coder_scratch(rows, wide):
    return pltpu.VMEM((rows, wide), F32)


class Decoder:
    def __init__(self, ref):
        self.ref = ref
        exponents = ref[:, ref.shape[1] - 128 :].astype(jnp.int32).astype(F32)
        self.scales = jnp.exp(exponents * OCTAVE) * (1 / LEVELS)

    def get(self, t, rows=slice(None)):
        levels = self.ref[rows, t * CN : (t + 1) * CN].astype(jnp.int32).astype(F32)
        return levels * self.scales[rows, t : t + 1]


def rows_of(shape):
    return jax.ShapeDtypeStruct(shape, F32)


def coded(rows, wide):
    return jax.ShapeDtypeStruct((rows, wide + 128), I16)


def call(kernel, operands, out_shape, scratch, flops, name, scalars=1):
    moved = sum(a.size * a.dtype.itemsize for a in (*operands, *out_shape))
    count = len(operands) - scalars
    return pl.pallas_call(
        kernel,
        in_specs=[pl.BlockSpec(memory_space=pltpu.SMEM)] * scalars
        + [pl.BlockSpec(memory_space=pltpu.VMEM)] * count,
        out_specs=[pl.BlockSpec(memory_space=pltpu.VMEM)] * len(out_shape),
        out_shape=out_shape,
        scratch_shapes=scratch,
        compiler_params=pltpu.CompilerParams(vmem_limit_bytes=VMEM_LIMIT),
        cost_estimate=pl.CostEstimate(
            flops=int(flops * WEIGHT), bytes_accessed=int(moved * WEIGHT), transcendentals=0
        ),
        name=name,
    )(*operands)


def product_lhs(z_xl, blocks, lhs):
    for k, f in enumerate(blocks):
        for zx in range(8):
            rel = zx ^ z_xl
            slot = k * 8 + (rel & 1) * 4 + (rel >> 1)
            lhs[pl.ds(pl.multiple_of(slot * 16, 16), 16), :] = f[zx * 16 : zx * 16 + 16]


def early_kernel(start, s_ref, f0, f1, i_ref, out, lhs):
    product_lhs(s_ref[1], (f0, f1), lhs)
    for t in range(out.shape[1] // TN):
        columns = slice(start + t * TN, start + (t + 1) * TN)
        sums = jnp.dot(lhs[...], i_ref[:, columns], preferred_element_type=F32)
        out[:, t * TN : (t + 1) * TN] = sums


def early(scalars, firsts, integrals, start, wide, name):
    return call(
        functools.partial(early_kernel, start),
        (scalars, *firsts, integrals),
        [rows_of((256, wide))],
        [pltpu.VMEM((256, NA_D), BF16)],
        2 * 256 * NA_D * wide,
        name,
    )[0]


def mirror_p_kernel(
    s_ref,
    f2,
    f3,
    early_ref,
    i_ref,
    keep_a,
    send_a,
    keep_b,
    send_b,
    lhs,
    sums,
    held_a,
    held_b,
):
    y_col = s_ref[0]
    product_lhs(s_ref[1], (f2, f3), lhs)
    coders = [Coder(held_a, send_a), Coder(held_b, send_b)]
    for t in range(P_WIDE // TN):
        columns = slice(t * TN, (t + 1) * TN)
        late = jnp.dot(lhs[...], i_ref[:, columns], preferred_element_type=F32)
        for k in range(2):
            rows = slice(k * 128, k * 128 + 128)
            sums[pl.ds(pl.multiple_of((k ^ y_col) * 128, 128), 128), :] = early_ref[rows, columns]
            sums[pl.ds(pl.multiple_of(((k + 2) ^ y_col) * 128, 128), 128), :] = late[rows]
        for part in range(TN // CN):
            half, tile = divmod(t * (TN // CN) + part, P_HALF // CN)
            y0, y1, y2, y3 = [
                sums[y * 128 : y * 128 + 128, part * CN : part * CN + CN] for y in range(4)
            ]
            place = slice(tile * CN, tile * CN + CN)
            if half == 0:
                keep_a[0:128, place], keep_a[128:256, place] = y0, y1
                coders[0].put(tile, jnp.concatenate([y3, y2]))
            else:
                keep_b[0:128, place], keep_b[128:256, place] = y0, y3
                coders[1].put(tile, jnp.concatenate([y1, y2]))
    for coder in coders:
        coder.end()


def mirror_p(scalars, firsts, first_sums, integrals):
    return call(
        mirror_p_kernel,
        (scalars, *firsts, first_sums, integrals),
        [rows_of((256, P_HALF)), coded(256, P_HALF)] * 2,
        [pltpu.VMEM((256, NA_D), BF16), pltpu.VMEM((OCC, TN), F32)]
        + [coder_scratch(256, P_HALF)] * 2,
        2 * 256 * NA_D * P_WIDE,
        "mirror_p",
    )


def mirror_q_kernel(s_ref, f2, f3, early_ref, i_ref, keep, send, lhs, sums, coding):
    y_col = s_ref[0]
    product_lhs(s_ref[1], (f2, f3), lhs)
    coder = Coder(coding, send)
    for t in range(Q_WIDE // TN):
        columns = slice(P_WIDE + t * TN, P_WIDE + (t + 1) * TN)
        late = jnp.dot(lhs[...], i_ref[:, columns], preferred_element_type=F32)
        for k in range(4):
            for xl in range(2):
                rows = slice((k % 2) * 128 + xl * 64, (k % 2) * 128 + xl * 64 + 64)
                place = pl.ds(pl.multiple_of(xl * 256 + (k ^ y_col) * 64, 64), 64)
                sums[place, :] = early_ref[rows, t * TN : (t + 1) * TN] if k < 2 else late[rows]
        keep[:, t * TN : (t + 1) * TN] = sums[0:256]
        for part in range(TN // CN):
            coder.put(t * (TN // CN) + part, sums[256:512, part * CN : part * CN + CN])
    coder.end()


def mirror_q(scalars, firsts, first_sums, integrals):
    return call(
        mirror_q_kernel,
        (scalars, *firsts, first_sums, integrals),
        [rows_of((256, Q_WIDE)), coded(256, Q_WIDE)],
        [
            pltpu.VMEM((256, NA_D), BF16),
            pltpu.VMEM((OCC, TN), F32),
            coder_scratch(256, Q_WIDE),
        ],
        2 * 256 * NA_D * Q_WIDE,
        "mirror_q",
    )


def direct_kernel(s_ref, n0, n1, n2, n3, i_ref, keep, send, lhs):
    y_col = s_ref[0]
    for place, n in enumerate((n0, n1, n2, n3)):
        for rel_y in range(4):
            slot = (rel_y ^ y_col) * 4 + place
            rows = pl.ds(pl.multiple_of(slot * 16, 16), 16)
            for k in range(CT):
                tile = pl.multiple_of(s_ref[2 + k] * TILE, TILE)
                lhs[rows, k * TILE : (k + 1) * TILE] = n[
                    rel_y * 16 : rel_y * 16 + 16, pl.ds(tile, TILE)
                ]
    for t in range(NA_D // TN):
        columns = slice(t * TN, (t + 1) * TN)
        sums = lax.dot_general(
            lhs[...], i_ref[columns, :], (((1,), (1,)), ((), ())), preferred_element_type=F32
        )
        keep[0:64, columns] = sums[0:64]
        send[0:64, columns] = sums[64:128]
        keep[64:128, columns] = sums[128:192]
        send[64:128, columns] = sums[192:256]


def direct(scalars, blocks, integrals, name):
    return call(
        direct_kernel,
        (scalars, *blocks, integrals),
        [rows_of((128, NA_D))] * 2,
        [pltpu.VMEM((256, NB_D), BF16)],
        2 * 256 * NA_D * NB_D,
        name,
    )


def fold_kernel(own, other, keep, *refs):
    sends, held = refs[:-1], refs[-1]
    other, coder = Decoder(other), Coder(held, *sends)
    height = keep.shape[0]
    for t in range(own.shape[1] // CN):
        total = own[:, t * CN : (t + 1) * CN] + other.get(t)
        keep[:, t * CN : (t + 1) * CN] = total[:height]
        coder.put(t, total[height:])
    coder.end()


def fold(own, other, count, name):
    rows, wide = own.shape
    height = rows // count
    return call(
        fold_kernel,
        (own, other),
        [rows_of((height, wide))] + [coded(height, wide)] * (count - 1),
        [coder_scratch(rows - height, wide)],
        0,
        name,
        scalars=0,
    )


def merge_kernel(a, a1, b, b1, keep, send, held):
    coder = Coder(held, send)
    for half, (own, other) in enumerate(((a, Decoder(a1)), (b, Decoder(b1)))):
        for t in range(P_HALF // CN):
            tile = half * (P_HALF // CN) + t
            total = own[:, t * CN : (t + 1) * CN] + other.get(t)
            keep[:, tile * CN : (tile + 1) * CN] = total[0:64]
            coder.put(tile, total[64:128])
    coder.end()


def merge(parts):
    return call(
        merge_kernel,
        parts,
        [rows_of((64, P_WIDE)), coded(64, P_WIDE)],
        [coder_scratch(64, P_WIDE)],
        0,
        "merge",
        scalars=0,
    )


def core_kernel(own, other, keep, send, held):
    coder = Coder(held, send)
    for t in range(NA_D // CN):
        columns = slice(t * CN, (t + 1) * CN)
        keep[:, columns] = own[0:64, columns] + other[0:64, columns]
        coder.put(t, own[64:128, columns] + other[64:128, columns])
    coder.end()


def core_fold(own, other, name):
    return call(
        core_kernel,
        (own, other),
        [rows_of((64, NA_D)), coded(64, NA_D)],
        [coder_scratch(64, NA_D)],
        0,
        name,
        scalars=0,
    )


PARTS = ((0, 1, 2, 6), (3, 7, 4, 5))


def finish_first_kernel(s_ref, k0, r0, k1, r1, o_ref):
    z_xl = s_ref[1]
    for rels, own, other in ((PARTS[0], k0, r0), (PARTS[1], k1, r1)):
        other = Decoder(other)
        for t in range(NA_D // CN):
            columns = slice(t * CN, (t + 1) * CN)
            total = (own[:, columns] + other.get(t)).astype(BF16)
            for part, rel in enumerate(rels):
                rows = pl.ds(pl.multiple_of((rel ^ z_xl) * 16, 16), 16)
                o_ref[rows, columns] = total[part * 16 : part * 16 + 16]


def finish_first(scalars, parts):
    return call(
        finish_first_kernel,
        (scalars, *parts),
        [jax.ShapeDtypeStruct((128, NA_D), BF16)],
        [],
        0,
        "finish_first",
    )[0]


def join_kernel(p, p1, q, q1, q2, q3, keep, send1, send2, send3, held):
    coder = Coder(held, send1, send2, send3)
    for start, own, others in ((0, p, (p1,)), (P_WIDE // CN, q, (q1, q2, q3))):
        others = [Decoder(r) for r in others]
        for t in range(own.shape[1] // CN):
            total = own[:, t * CN : (t + 1) * CN]
            for other in others:
                total = total + other.get(t)
            keep[:, (start + t) * CN : (start + t + 1) * CN] = total[0:16]
            coder.put(start + t, total[16:64])
    coder.end()


def join(p, q):
    return call(
        join_kernel,
        (*p, *q),
        [rows_of((16, NB_D))] + [coded(16, NB_D)] * 3,
        [coder_scratch(48, NB_D)],
        0,
        "join",
        scalars=0,
    )


def finish_second_kernel(own, r1, r2, r3, o_ref):
    others = [Decoder(r) for r in (r1, r2, r3)]
    for t in range(NB_D // CN):
        total = own[:, t * CN : (t + 1) * CN]
        for other in others:
            total = total + other.get(t)
        o_ref[:, t * CN : (t + 1) * CN] = total.astype(BF16)


def finish_second(parts):
    return call(
        finish_second_kernel,
        parts,
        [jax.ShapeDtypeStruct((16, NB_D), BF16)],
        [],
        0,
        "finish_second",
        scalars=0,
    )[0]


def together(*values):
    return lax.optimization_barrier(values)


def on_device(amp_first, amp_second, integrals, tile_order):
    row, col = lax.axis_index("row"), lax.axis_index("col")
    place = jnp.stack([(row // 8) ^ col, row % 8]).astype(jnp.int32)
    scalars = jnp.concatenate([place, tile_order[0]])

    second = amp_second
    first_xh = swap("first", amp_first, xh=1)
    first_core = swap("first", amp_first, core=1)
    y1, y2, y3 = [swap("second", second, y=r) for r in (1, 2, 3)]
    sums_p = early(scalars, (amp_first, first_core), integrals, 0, P_WIDE, "early_p")
    sums_q = early(scalars, (amp_first, first_core), integrals, P_WIDE, Q_WIDE, "early_q")
    y1, y2, y3, scalars, sums_p = together(y1, y2, y3, scalars, sums_p)
    n0 = jnp.concatenate([second, y1, y2, y3])
    first_both = swap("first", first_xh, core=1)
    x0 = swap("n", n0, xl=1)
    n1, n3 = swap("n", n0, z=1), swap("n", n0, z=3)
    pa, pa_send, pb, pb_send = mirror_p(scalars, (first_xh, first_both), sums_p, integrals)
    pa_got, pb_got = swap("pa", pa_send, y=3), swap("pb", pb_send, y=1)
    pa, pb, sums_q, first_xh, first_both = together(pa, pb, sums_q, first_xh, first_both)
    q, q_send = mirror_q(scalars, (first_xh, first_both), sums_q, integrals)
    n0, x0, n1, n3, q, q_send = together(n0, x0, n1, n3, q, q_send)
    q_got = swap("q", q_send, xl=1)
    x1, x3 = swap("x", x0, z=1), swap("x", x0, z=3)
    keep0, send0 = direct(scalars, (n0, x0, n1, n3), integrals, "direct_0")
    pa, pa_got, pb, pb_got = together(pa, pa_got, pb, pb_got)
    pa, pa_send = fold(pa, pa_got, 2, "fold_pa")
    pb, pb_send = fold(pb, pb_got, 2, "fold_pb")
    pa_got, pb_got = swap("pa", pa_send, y=1), swap("pb", pb_send, y=3)
    got0 = swap("chunk0", send0, core=1)
    n3, x1, x3, pa, pb = together(n3, x1, x3, pa, pb)
    q = fold(q, q_got, 4, "fold_q_xl")
    n2, x2 = swap("n3", n3, z=1), swap("x1", x1, z=3)
    p, p_send = merge((pa, pa_got, pb, pb_got))
    p, p_send, *q = together(p, p_send, *q)
    p_got = swap("p", p_send, xl=1)
    q_got = [swap("q", q[r], y=r) for r in (1, 2, 3)]
    keep0, send0 = core_fold(keep0, got0, "core_0")
    got0 = swap("chunk0", send0, xh=1)
    x1, x3, n2, x2, p = together(x1, x3, n2, x2, p)
    keep1, send1 = direct(scalars, (x1, x3, n2, x2), integrals, "direct_1")
    p_got, keep1, send1, *q_got = together(p_got, keep1, send1, *q_got)
    parts = join((p, p_got), (q[0], *q_got))
    got1 = swap("chunk1", send1, core=1)
    keep1, got1, *parts = together(keep1, got1, *parts)
    parts = [parts[0]] + [swap("z", parts[r], z=r) for r in (1, 2, 3)]
    keep1, send1 = core_fold(keep1, got1, "core_1")
    got1 = swap("chunk1", send1, xh=1)
    ladder_first = finish_first(scalars, (keep0, got0, keep1, got1))
    ladder_first, *parts = together(ladder_first, *parts)
    ladder_second = finish_second(parts)
    return ladder_first, ladder_second


def solution(mesh):
    in_specs = (P("col", "row"), P("row", "col"), P("row", "col"), P("col", None))
    out_specs = (P("col", "row"), P("row", "col"))
    return jax.shard_map(
        on_device, mesh=mesh, in_specs=in_specs, out_specs=out_specs, check_vma=False
    )
```
